32 devices in a mesh: branch: 8 (over z, x), sub: 4 (over y, core).
Axes of the slice: x: 2, y: 2, z: 4, core: 2. Of those that a mesh axis runs over, the one named last changes fastest.
Arguments:
- vectors: float32 [1152, 16, 128], P(('branch', 'sub')), may hold values from -6 to 6
- leaf_basis: float32 [1152, 64, 128], P(('branch', 'sub')), may hold values from -0.5 to 0.5
- near_index: int32 [1152, 3], P(('branch', 'sub')), may hold values from 0 to 1151, as said below
- near_blocks: float32 [1152, 3, 128, 128], P(('branch', 'sub')), may hold values from -0.3125 to 0.3125
- coupling_index: int32 [1152, 4], P(('branch', 'sub')), may hold values from 0 to 1151, as said below
- coupling_blocks: float32 [1152, 4, 64, 64], P(('branch', 'sub')), may hold values from -0.375 to 0.375
- leaf_transfer: float32 [1152, 64, 64], P(('branch', 'sub')), may hold values from -0.125 to 0.125
- cluster_transfer: float32 [32, 64, 64], P(('branch', 'sub')), may hold values from -0.375 to 0.375
- branch_index: int32 [8, 4], P('branch'), may hold values from 0 to 7, as said below
- branch_blocks: float32 [8, 4, 64, 64], P('branch'), may hold values from -0.375 to 0.375
Outputs:
- product: float32 [1152, 16, 128], P(('branch', 'sub'))
The draws below stay inside these ranges and needn't reach their ends.
Inputs may be any that keep to these rules, and one draw needn't show every extreme that they name: `near_index`: entry 0 of row l is l itself; every entry of row l lies within 36 of l. `coupling_index`: every entry of row l lies within 36 of l. `branch_index`: the entries of a row are distinct and differ from the row's own branch cluster.
All inputs are finite; a program needn't handle non-finite values.
Results may differ from the reference program's by a relative error of at most 0.000067.
Values sent between devices are 32-bit elements; how exact they have to be, the bound alone decides.
No kernel may reach another device: no remote copies, remote signals or barrier semaphores. Data moves between devices by JAX's collectives and lax.ppermute only.
A program may use at most 64 MiB of HBM per device.

```python
import jax
import jax.numpy as jnp
from jax import lax

P_SIZE = 128
R = 64
NV = 16
LEAF_DEV = 36
NEAR = 3
COUP = 4
HALO = 36
MEMBERS = 4
BRANCHES = 8
LEAVES = 1152
TOP_COUP = 4


def within_reach(key, columns):
    offsets = jax.random.randint(key, (LEAVES, columns), -HALO, HALO + 1, dtype=jnp.int32)
    rows = jnp.arange(LEAVES, dtype=jnp.int32)[:, None]
    return jnp.clip(rows + offsets, 0, LEAVES - 1).astype(jnp.int32)


def draw_near_index(key, part):
    listed = within_reach(jax.random.fold_in(key, 11), NEAR)
    rows = jnp.arange(LEAVES, dtype=jnp.int32)
    return listed.at[:, 0].set(rows)


def draw_coupling_index(key, part):
    return within_reach(jax.random.fold_in(key, 23), COUP)


def draw_branch_index(key, part):
    keys = jax.random.split(jax.random.fold_in(key, 37), BRANCHES)
    offsets = jax.vmap(lambda one: jax.random.permutation(one, BRANCHES - 1)[:TOP_COUP])(keys) + 1
    rows = jnp.arange(BRANCHES, dtype=jnp.int32)[:, None]
    return ((rows + offsets.astype(jnp.int32)) % BRANCHES).astype(jnp.int32)


def block_scale(rng, shape, shards, smallest, top_value):
    def one(dim, parts):
        steps = jax.random.uniform(jax.random.fold_in(jax.random.fold_in(rng, 6), dim), (parts,), jnp.float32, smallest / len(shards), top_value / len(shards))
        return jnp.repeat(jnp.exp(steps), shape[dim] // parts).reshape((-1,) + (1,) * (len(shape) - dim - 1))

    loudness = one(*shards[0])
    for cut in shards[1:]:
        loudness = loudness * one(*cut)
    return loudness


def bell_draw(key, dims, deviation, reach, cuts=(), held_as=jnp.bfloat16):
    entries = jax.random.normal(key, dims, jnp.float32) * deviation
    if len(cuts) > 0:
        entries = block_scale(key, dims, cuts, -0.22, 0.18) * entries
    return jnp.clip(entries, min=-reach, max=reach).astype(held_as)


def setup_inputs(seed: int = 0) -> dict:
    splits = jax.random.split(jax.random.key(seed), 11)
    vectors = bell_draw(splits[0], (LEAVES, NV, P_SIZE), 1.0, 6.0, ((0, 32),), jnp.float32)
    leaf_basis = bell_draw(splits[1], (LEAVES, R, P_SIZE), P_SIZE ** -0.5, 0.5, ((0, 32),), jnp.float32)
    near_index = draw_near_index(jax.random.fold_in(splits[10], 71), 0)
    near_blocks = bell_draw(splits[3], (LEAVES, NEAR, P_SIZE, P_SIZE), (NEAR * P_SIZE) ** -0.5, 0.3125, ((0, 32),), jnp.float32)
    coupling_index = draw_coupling_index(jax.random.fold_in(splits[10], 71), 0)
    coupling_blocks = bell_draw(splits[5], (LEAVES, COUP, R, R), (COUP * R) ** -0.5, 0.375, ((0, 32),), jnp.float32)
    leaf_transfer = bell_draw(splits[6], (LEAVES, R, R), (R * LEAF_DEV) ** -0.5, 0.125, ((0, 32),), jnp.float32)
    cluster_transfer = bell_draw(splits[7], (LEAVES // LEAF_DEV, R, R), (R * MEMBERS) ** -0.5, 0.375, ((0, 32),), jnp.float32)
    branch_index = draw_branch_index(jax.random.fold_in(splits[10], 71), 0)
    branch_blocks = bell_draw(splits[9], (BRANCHES, TOP_COUP, R, R), (R * TOP_COUP) ** -0.5, 0.375, ((0, 8),), jnp.float32)
    return dict(vectors=vectors, leaf_basis=leaf_basis, near_index=near_index, near_blocks=near_blocks, coupling_index=coupling_index, coupling_blocks=coupling_blocks, leaf_transfer=leaf_transfer, cluster_transfer=cluster_transfer, branch_index=branch_index, branch_blocks=branch_blocks)


highest = lax.Precision.HIGHEST


def reference(vectors, leaf_basis, near_index, near_blocks, coupling_index, coupling_blocks, leaf_transfer, cluster_transfer, branch_index, branch_blocks):
    clusters = LEAVES // LEAF_DEV
    coeffs = jnp.einsum('lrp,lvp->lvr', leaf_basis, vectors, precision=highest)
    near_rows = vectors[near_index]
    near_part = jnp.einsum('lkpq,lkvq->lvp', near_blocks, near_rows, precision=highest)
    leaf_far = jnp.einsum('lkrs,lkvs->lvr', coupling_blocks, coeffs[coupling_index], precision=highest)
    grouped_transfer = leaf_transfer.reshape(clusters, LEAF_DEV, R, R)
    cluster = jnp.einsum('dcrs,dcvs->dvr', grouped_transfer, coeffs.reshape(clusters, LEAF_DEV, NV, R), precision=highest)
    grouped_cluster = cluster_transfer.reshape(BRANCHES, MEMBERS, R, R)
    node = jnp.einsum('bsrt,bsvt->bvr', grouped_cluster, cluster.reshape(BRANCHES, MEMBERS, NV, R), precision=highest)
    branch_far = jnp.einsum('bkrs,bkvs->bvr', branch_blocks, node[branch_index], precision=highest)
    cluster_down = jnp.einsum('bsrt,bvr->bsvt', grouped_cluster, branch_far, precision=highest).reshape(clusters, NV, R)
    leaf_total = leaf_far + jnp.einsum('dcrs,dvr->dcvs', grouped_transfer, cluster_down, precision=highest).reshape(LEAVES, NV, R)
    return near_part + jnp.einsum('lrp,lvr->lvp', leaf_basis, leaf_total, precision=highest)
```

```python
import jax
import jax.numpy as jnp
from jax import lax
from jax.experimental import pallas as pl
from jax.experimental.pallas import tpu as pltpu
from jax.sharding import PartitionSpec as P

AXES = ("branch", "sub")
f32, bf16 = jnp.float32, jnp.bfloat16
VMEM = pl.BlockSpec(memory_space=pltpu.VMEM)
SMEM = pl.BlockSpec(memory_space=pltpu.SMEM)
ANY = pl.BlockSpec(memory_space=pl.ANY)
PARAMS = pltpu.CompilerParams(vmem_limit_bytes=16 * 1024 * 1024)
CHUNKS = 2


def halves(x):
    high = x.astype(bf16)
    return high, (x - high.astype(f32)).astype(bf16)


def rows_of(x):
    high, low = halves(x)
    return jnp.concatenate(
        [jnp.concatenate([high, high], axis=1), jnp.concatenate([low, jnp.zeros_like(low)], axis=1)], axis=0
    )


def weights_of(w, axis):
    return jnp.concatenate(halves(w), axis=axis)


def both(x):
    n = x.shape[0] // 2
    return x[:n] + x[n:]


def dot_nt(a, b):
    return lax.dot_general(a, b, (((1,), (1,)), ((), ())), preferred_element_type=f32)


def dot_nn(a, b):
    return lax.dot_general(a, b, (((1,), (0,)), ((), ())), preferred_element_type=f32)


def pack(x):
    n = x.shape[0] // 2
    return jnp.concatenate([x[:n], x[n:]], axis=1)


def unpack(x):
    w = x.shape[1] // 2
    return jnp.concatenate([x[:, :w], x[:, w:]], axis=0)


def stream(sources, targets, sems):
    chunks = sems.shape[0]
    size = targets[0].shape[0] // chunks
    parts = []
    for c in range(chunks):
        part = pl.ds(c * size, size)
        copies = [
            pltpu.make_async_copy(src.at[part], dst.at[part], sems.at[c, i])
            for i, (src, dst) in enumerate(zip(sources, targets))
        ]
        for copy in copies:
            copy.start()
        parts.append((range(c * size, (c + 1) * size), copies))
    return parts


def wait_all(copies):
    for copy in copies:
        copy.wait()


def three(dot, a, weight):
    n = a.shape[0]
    rows = jnp.concatenate(halves(a), axis=0)
    high, low = halves(weight)
    wide = dot(rows, high)
    return wide[:n] + wide[n:] + dot(rows[:n], low)


def up_kernel(
    vectors_hbm, basis_hbm, transfer_hbm, top_hbm, blocks_hbm,
    share, folded, vectors, basis, blocks, transfer, top, sems, top_sem, block_sem,
):
    leaves, rank, points = basis.shape
    parts = stream((basis_hbm, transfer_hbm, vectors_hbm), (basis, transfer, vectors), sems)
    top_copy = pltpu.make_async_copy(top_hbm, top, top_sem)
    top_copy.start()
    block_copy = pltpu.make_async_copy(blocks_hbm.at[:, 0], blocks, block_sem)
    block_copy.start()
    for part, copies in parts:
        wait_all(copies)
        for l in part:
            high, low = halves(three(dot_nn, transfer[l], basis[l]))
            folded[l // 2, :, (l % 2) * points : (l % 2 + 1) * points] = jnp.concatenate([high, low, high], axis=0)
    cluster = None
    for first in range(0, leaves, 2):
        rows, weights = [], []
        for l in (first, first + 1):
            lane = pl.ds((l % 2) * points, points)
            weights += [folded[l // 2, :rank, lane], folded[l // 2, rank : 2 * rank, lane]]
            rows.append(rows_of(vectors[l]))
        term = dot_nt(jnp.concatenate(rows, axis=1), jnp.concatenate(weights, axis=1))
        cluster = term if cluster is None else cluster + term
    top_copy.wait()
    share[...] = pack(three(dot_nt, both(cluster), top[0]))
    block_copy.wait()


def coeffs_kernel(vectors, basis, coeffs):
    half = coeffs.shape[0]
    for j in range(half):
        pair = [both(dot_nt(rows_of(vectors[l]), weights_of(basis[l], 1))) for l in (j, j + half)]
        coeffs[j] = jnp.concatenate(pair, axis=1)


def sides(own, across, beside):
    n = own[1]
    odd = lax.rem(lax.axis_index("sub"), 2)
    return (own[0], n), (beside, 2 * n * (1 - odd)), (across, 2 * n * odd)


def first_leaf(leaves):
    return (lax.axis_index("branch") * lax.axis_size("sub") + lax.axis_index("sub")) * leaves - leaves


def turned_sum(rows, blocks):
    weights = jnp.concatenate([weights_of(block, 1) for block in blocks], axis=1)
    return both(dot_nt(weights, jnp.concatenate(rows, axis=1)).T)


def own_kernel(vectors, blocks, next_hbm, out, next_blocks, sem):
    copy = pltpu.make_async_copy(next_hbm, next_blocks, sem)
    copy.start()
    for l in range(blocks.shape[0]):
        out[l] = turned_sum([rows_of(vectors[l])], [blocks[l]])
    copy.wait()


def coupling_kernel(index, coeffs, across, beside, basis, near, blocks, next_hbm, out, next_blocks, split, far, sem):
    leaves, coup, rank = blocks.shape[:3]
    copy = pltpu.make_async_copy(next_hbm.at[:, pl.ds(1, next_blocks.shape[1])], next_blocks, sem)
    copy.start()
    half = leaves // 2
    left = lax.broadcasted_iota(jnp.int32, coeffs.shape[1:], 1) < rank
    for ref, base in sides((coeffs, leaves), across, beside):
        for j in range(half):
            two = ref[j]
            turned = pltpu.roll(two, rank, 1)
            for l, twice in ((j, jnp.where(left, two, turned)), (j + half, jnp.where(left, turned, two))):
                high = twice.astype(bf16)
                low = jnp.where(left, twice - high.astype(f32), 0.0).astype(bf16)
                split[base + l] = jnp.concatenate([high, low], axis=0)
    anchor = first_leaf(leaves)
    for l in range(leaves):
        rows = jnp.concatenate([split[index[k, l] - anchor] for k in range(coup)], axis=1)
        weights = jnp.concatenate([weights_of(blocks[l, k], 1) for k in range(coup)], axis=1)
        far[l] = both(dot_nt(rows, weights))
    for l in range(leaves):
        out[l] = near[l] + three(dot_nn, far[l], basis[l])
    copy.wait()


def last_kernel(
    near_index, branch_index, vectors, across, beside, nodes, branch_blocks, top, folded, partial, blocks, out, split
):
    leaves, others, points = blocks.shape[:3]
    branch = lax.axis_index("branch")
    far = None
    for k in range(branch_blocks.shape[1]):
        node = unpack(nodes[jnp.bitwise_xor(branch_index[0, k], branch)])
        term = three(dot_nt, node, branch_blocks[0, k])
        far = term if far is None else far + term
    high, low = halves(three(dot_nn, far, top[0]))
    down = jnp.concatenate([high, high, low], axis=1)
    for ref, base in sides((vectors, leaves), across, beside):
        for l in range(leaves):
            split[base + l] = rows_of(ref[l])
    anchor = first_leaf(leaves)
    for l in range(leaves):
        if l % 2 == 0:
            two = dot_nn(down, folded[l // 2])
        rows = [split[near_index[k + 1, l] - anchor] for k in range(others)]
        near = turned_sum(rows, [blocks[l, k] for k in range(others)])
        out[l] = partial[l] + near + two[:, (l % 2) * points : (l % 2 + 1) * points]


def in_hbm(*arrays):
    return [pltpu.with_memory_space_constraint(x, pltpu.HBM) for x in arrays]


def flip(x, mask, count):
    return lax.ppermute(x, AXES, [(i, i ^ mask) for i in range(count)])


def across_chips(beside, count):
    pairs = [(i, i + 2) for i in range(0, count - 2, 2)] + [(i + 3, i + 1) for i in range(0, count - 2, 2)]
    return lax.ppermute(beside, AXES, pairs + [(count - 2, count - 1), (1, 0)])


def per_device(
    vectors,
    leaf_basis,
    near_index,
    near_blocks,
    coupling_index,
    coupling_blocks,
    leaf_transfer,
    cluster_transfer,
    branch_index,
    branch_blocks,
):
    leaves, nv, points = vectors.shape
    rank = leaf_basis.shape[1]
    near = near_blocks.shape[1]
    half = leaves // 2
    members, branches = lax.axis_size("sub"), lax.axis_size("branch")
    count = members * branches
    sds = jax.ShapeDtypeStruct
    product = sds((leaves, nv, points), f32)

    vec_beside = flip(vectors, 1, count)

    share, folded, vectors_in, basis_in, own_blocks = pl.pallas_call(
        up_kernel,
        out_shape=(
            sds((nv // 2, 2 * rank), f32),
            sds((half, 3 * rank, 2 * points), bf16),
            product,
            sds(leaf_basis.shape, f32),
            sds((leaves, points, points), f32),
        ),
        in_specs=[ANY] * 5,
        out_specs=(VMEM,) * 5,
        scratch_shapes=[
            pltpu.VMEM(leaf_transfer.shape, f32),
            pltpu.VMEM(cluster_transfer.shape, f32),
            pltpu.SemaphoreType.DMA((CHUNKS, 3)),
            pltpu.SemaphoreType.DMA,
            pltpu.SemaphoreType.DMA,
        ],
        compiler_params=PARAMS,
        name="up",
    )(*in_hbm(vectors, leaf_basis, leaf_transfer, cluster_transfer, near_blocks))

    node = share + flip(share, 1, count)

    coeffs = pl.pallas_call(
        coeffs_kernel,
        out_shape=sds((half, nv, 2 * rank), f32),
        in_specs=[VMEM] * 2,
        out_specs=VMEM,
        compiler_params=PARAMS,
        name="coeffs",
    )(vectors_in, basis_in)
    coeff_beside = flip(coeffs, 1, count)
    coeff_across = across_chips(coeff_beside, count)
    vec_across = across_chips(vec_beside, count)

    bit = 2
    while bit < members:
        node = node + flip(node, bit + 1, count)
        bit *= 2
    nodes = node[None]
    while bit < count:
        nodes = jnp.concatenate([nodes, flip(nodes, bit + 1, count)], axis=0)
        bit *= 2

    own, coup_blocks = pl.pallas_call(
        own_kernel,
        out_shape=(product, sds(coupling_blocks.shape, f32)),
        in_specs=[VMEM, VMEM, ANY],
        out_specs=(VMEM, VMEM),
        scratch_shapes=[pltpu.SemaphoreType.DMA],
        compiler_params=PARAMS,
        name="near_own",
    )(vectors_in, own_blocks, *in_hbm(coupling_blocks))

    partial, other_blocks = pl.pallas_call(
        coupling_kernel,
        out_shape=(product, sds((leaves, near - 1, points, points), f32)),
        in_specs=[SMEM] + [VMEM] * 6 + [ANY],
        out_specs=(VMEM, VMEM),
        scratch_shapes=[
            pltpu.VMEM((3 * leaves, 2 * nv, 2 * rank), bf16),
            pltpu.VMEM((leaves, nv, rank), f32),
            pltpu.SemaphoreType.DMA,
        ],
        compiler_params=PARAMS,
        name="coupling",
    )(coupling_index.T, coeffs, coeff_across, coeff_beside, basis_in, own, coup_blocks, *in_hbm(near_blocks))

    return pl.pallas_call(
        last_kernel,
        out_shape=product,
        in_specs=[SMEM] * 2 + [VMEM] * 9,
        out_specs=VMEM,
        scratch_shapes=[pltpu.VMEM((3 * leaves, 2 * nv, 2 * points), bf16)],
        compiler_params=PARAMS,
        name="last",
    )(
        near_index.T, branch_index, vectors_in, vec_across, vec_beside, nodes, branch_blocks, cluster_transfer,
        folded, partial, other_blocks,
    )


def solution(mesh):
    lead = P(AXES)
    in_specs = (lead,) * 8 + (P("branch"),) * 2
    return jax.shard_map(per_device, mesh=mesh, in_specs=in_specs, out_specs=lead, check_vma=False)
```

```python
import jax
import jax.numpy as jnp
from jax import lax
from jax.experimental import pallas as pl
from jax.experimental.pallas import tpu as pltpu
from jax.sharding import PartitionSpec as P

AXES = ("branch", "sub")
f32, bf16 = jnp.float32, jnp.bfloat16
VMEM = pl.BlockSpec(memory_space=pltpu.VMEM)
SMEM = pl.BlockSpec(memory_space=pltpu.SMEM)
ANY = pl.BlockSpec(memory_space=pl.ANY)
PARAMS = pltpu.CompilerParams(vmem_limit_bytes=16 * 1024 * 1024)
CHUNKS = 2


def halves(x):
    high = x.astype(bf16)
    return high, (x - high.astype(f32)).astype(bf16)


def rows_of(x):
    high, low = halves(x)
    return jnp.concatenate(
        [jnp.concatenate([high, high], axis=1), jnp.concatenate([low, jnp.zeros_like(low)], axis=1)], axis=0
    )


def weights_of(w, axis):
    return jnp.concatenate(halves(w), axis=axis)


def both(x):
    n = x.shape[0] // 2
    return x[:n] + x[n:]


def dot_nt(a, b):
    return lax.dot_general(a, b, (((1,), (1,)), ((), ())), preferred_element_type=f32)


def dot_nn(a, b):
    return lax.dot_general(a, b, (((1,), (0,)), ((), ())), preferred_element_type=f32)


def pack(x):
    n = x.shape[0] // 2
    return jnp.concatenate([x[:n], x[n:]], axis=1)


def unpack(x):
    w = x.shape[1] // 2
    return jnp.concatenate([x[:, :w], x[:, w:]], axis=0)


def stream(sources, targets, sems):
    chunks = sems.shape[0]
    size = targets[0].shape[0] // chunks
    parts = []
    for c in range(chunks):
        part = pl.ds(c * size, size)
        copies = [
            pltpu.make_async_copy(src.at[part], dst.at[part], sems.at[c, i])
            for i, (src, dst) in enumerate(zip(sources, targets))
        ]
        for copy in copies:
            copy.start()
        parts.append((range(c * size, (c + 1) * size), copies))
    return parts


def then(body):
    pl.when(lax.axis_index("sub") >= 0)(body)


def wait_all(copies):
    for copy in copies:
        copy.wait()


def three(dot, a, weight):
    n = a.shape[0]
    rows = jnp.concatenate(halves(a), axis=0)
    high, low = halves(weight)
    wide = dot(rows, high)
    return wide[:n] + wide[n:] + dot(rows[:n], low)


def up_kernel(
    vectors_hbm, basis_hbm, transfer_hbm, top_hbm, blocks_hbm,
    share, folded, vectors, basis, blocks, transfer, top, sems, top_sem, block_sem,
):
    leaves, rank, points = basis.shape
    parts = stream((basis_hbm, transfer_hbm, vectors_hbm), (basis, transfer, vectors), sems)
    top_copy = pltpu.make_async_copy(top_hbm, top, top_sem)
    top_copy.start()
    block_copy = pltpu.make_async_copy(blocks_hbm.at[:, 0], blocks, block_sem)
    block_copy.start()

    @then
    def _():
        cluster = None
        for part, copies in parts:
            wait_all(copies)
            for l in part:
                high, low = halves(three(dot_nn, transfer[l], basis[l]))
                folded[l // 2, :, (l % 2) * points : (l % 2 + 1) * points] = jnp.concatenate([high, low, high], axis=0)
            for first in part[::2]:
                rows, weights = [], []
                for l in (first, first + 1):
                    lane = pl.ds((l % 2) * points, points)
                    weights += [folded[l // 2, :rank, lane], folded[l // 2, rank : 2 * rank, lane]]
                    rows.append(rows_of(vectors[l]))
                term = dot_nt(jnp.concatenate(rows, axis=1), jnp.concatenate(weights, axis=1))
                cluster = term if cluster is None else cluster + term
        top_copy.wait()
        share[...] = pack(three(dot_nt, both(cluster), top[0]))

    block_copy.wait()


def coeffs_kernel(vectors, basis, coeffs):
    half = coeffs.shape[0]
    for j in range(half):
        pair = [both(dot_nt(rows_of(vectors[l]), weights_of(basis[l], 1))) for l in (j, j + half)]
        coeffs[j] = jnp.concatenate(pair, axis=1)


def sides(own, across, beside):
    n = own[1]
    odd = lax.rem(lax.axis_index("sub"), 2)
    return (own[0], n), (beside, 2 * n * (1 - odd)), (across, 2 * n * odd)


def first_leaf(leaves):
    return (lax.axis_index("branch") * lax.axis_size("sub") + lax.axis_index("sub")) * leaves - leaves


def turned_sum(rows, blocks):
    weights = jnp.concatenate([weights_of(block, 1) for block in blocks], axis=1)
    return both(dot_nt(weights, jnp.concatenate(rows, axis=1)).T)


def own_kernel(vectors, blocks, next_hbm, out, next_blocks, sem):
    count, others = next_blocks.shape[:2]
    copy = pltpu.make_async_copy(next_hbm.at[pl.ds(0, count), pl.ds(1, others)], next_blocks, sem)
    copy.start()

    @then
    def _():
        for l in range(blocks.shape[0]):
            out[l] = turned_sum([rows_of(vectors[l])], [blocks[l]])

    copy.wait()


def coupling_kernel(
    index, coeffs, across, beside, basis, near, blocks, next_hbm, out, next_blocks, split, far, sem
):
    leaves, (coup, rank) = basis.shape[0], blocks.shape[1:3]
    count, others = next_blocks.shape[:2]
    copy = pltpu.make_async_copy(next_hbm.at[pl.ds(leaves - count, count), pl.ds(1, others)], next_blocks, sem)
    copy.start()

    @then
    def _():
        half = leaves // 2
        left = lax.broadcasted_iota(jnp.int32, coeffs.shape[1:], 1) < rank
        for ref, base in sides((coeffs, leaves), across, beside):
            for j in range(half):
                two = ref[j]
                turned = pltpu.roll(two, rank, 1)
                for l, twice in ((j, jnp.where(left, two, turned)), (j + half, jnp.where(left, turned, two))):
                    high = twice.astype(bf16)
                    low = jnp.where(left, twice - high.astype(f32), 0.0).astype(bf16)
                    split[base + l] = jnp.concatenate([high, low], axis=0)
        anchor = first_leaf(leaves)
        for l in range(leaves):
            rows = jnp.concatenate([split[index[k, l] - anchor] for k in range(coup)], axis=1)
            weights = jnp.concatenate([weights_of(blocks[l, k], 1) for k in range(coup)], axis=1)
            far[l] = both(dot_nt(rows, weights))
        for l in range(leaves):
            out[l] = near[l] + three(dot_nn, far[l], basis[l])

    copy.wait()


def last_kernel(
    near_index, branch_index, vectors, across, beside, nodes, far_nodes, branch_blocks, top, folded, partial, first_blocks,
    blocks, out, split,
):
    leaves, early, (others, points) = out.shape[0], first_blocks.shape[0], blocks.shape[1:3]
    branch = lax.axis_index("branch")
    known = nodes.shape[0]
    far = None
    for k in range(branch_blocks.shape[1]):
        slot = jnp.bitwise_xor(branch_index[0, k], branch)
        place = lax.rem(slot, known)
        node = unpack(jnp.where(slot < known, nodes[place], far_nodes[place]))
        term = three(dot_nt, node, branch_blocks[0, k])
        far = term if far is None else far + term
    high, low = halves(three(dot_nn, far, top[0]))
    down = jnp.concatenate([high, high, low], axis=1)
    for ref, base in sides((vectors, leaves), across, beside):
        for l in range(leaves):
            split[base + l] = rows_of(ref[l])
    anchor = first_leaf(leaves)
    for l in range(leaves):
        if l % 2 == 0:
            two = dot_nn(down, folded[l // 2])
        rows = [split[near_index[k + 1, l] - anchor] for k in range(others)]
        block = first_blocks.at[l] if l < early else blocks.at[l - early]
        near = turned_sum(rows, [block[k] for k in range(others)])
        out[l] = partial[l] + near + two[:, (l % 2) * points : (l % 2 + 1) * points]


def in_hbm(*arrays):
    return [pltpu.with_memory_space_constraint(x, pltpu.HBM) for x in arrays]


def flip(x, mask, count):
    return lax.ppermute(x, AXES, [(i, i ^ mask) for i in range(count)])


def across_chips(beside, count):
    pairs = [(i, i + 2) for i in range(0, count - 2, 2)] + [(i + 3, i + 1) for i in range(0, count - 2, 2)]
    return lax.ppermute(beside, AXES, pairs + [(count - 2, count - 1), (1, 0)])


def per_device(
    vectors,
    leaf_basis,
    near_index,
    near_blocks,
    coupling_index,
    coupling_blocks,
    leaf_transfer,
    cluster_transfer,
    branch_index,
    branch_blocks,
):
    leaves, nv, points = vectors.shape
    rank = leaf_basis.shape[1]
    near = near_blocks.shape[1]
    half = leaves // 2
    members, branches = lax.axis_size("sub"), lax.axis_size("branch")
    count = members * branches
    sds = jax.ShapeDtypeStruct
    product = sds((leaves, nv, points), f32)

    vec_beside = flip(vectors, 1, count)

    share, folded, vectors_in, basis_in, own_blocks = pl.pallas_call(
        up_kernel,
        out_shape=(
            sds((nv // 2, 2 * rank), f32),
            sds((half, 3 * rank, 2 * points), bf16),
            product,
            sds(leaf_basis.shape, f32),
            sds((leaves, points, points), f32),
        ),
        in_specs=[ANY] * 5,
        out_specs=(VMEM,) * 5,
        scratch_shapes=[
            pltpu.VMEM(leaf_transfer.shape, f32),
            pltpu.VMEM(cluster_transfer.shape, f32),
            pltpu.SemaphoreType.DMA((CHUNKS, 3)),
            pltpu.SemaphoreType.DMA,
            pltpu.SemaphoreType.DMA,
        ],
        compiler_params=PARAMS,
        name="up",
    )(*in_hbm(vectors, leaf_basis, leaf_transfer, cluster_transfer, near_blocks))

    share, coupling_blocks = lax.optimization_barrier((share, coupling_blocks))
    first = flip(share, 1, count)
    coeffs = pl.pallas_call(
        coeffs_kernel,
        out_shape=sds((half, nv, 2 * rank), f32),
        in_specs=[VMEM] * 2,
        out_specs=VMEM,
        compiler_params=PARAMS,
        name="coeffs",
    )(vectors_in, basis_in)
    coeff_beside = flip(coeffs, 1, count)
    node = share + first
    node, coeffs = lax.optimization_barrier((node, coeffs))
    early = 2 * (leaves // 3)
    own, first_blocks = pl.pallas_call(
        own_kernel,
        out_shape=(product, sds((early, near - 1, points, points), f32)),
        in_specs=[VMEM] * 2 + [ANY],
        out_specs=(VMEM, VMEM),
        scratch_shapes=[pltpu.SemaphoreType.DMA],
        compiler_params=PARAMS,
        name="near_own",
    )(vectors_in, own_blocks, *in_hbm(near_blocks))

    bit = 2
    while bit < members:
        node = node + flip(node, bit + 1, count)
        bit *= 2
    coeff_across = across_chips(coeff_beside, count)
    nodes = node[None]
    vec_across = across_chips(vec_beside, count)
    while 2 * bit < count:
        nodes = jnp.concatenate([nodes, flip(nodes, bit + 1, count)], axis=0)
        bit *= 2
    nodes, own = lax.optimization_barrier((nodes, own))
    far_nodes = flip(nodes, bit + 1, count)

    partial, other_blocks = pl.pallas_call(
        coupling_kernel,
        out_shape=(product, sds((leaves - early, near - 1, points, points), f32)),
        in_specs=[SMEM] + [VMEM] * 6 + [ANY],
        out_specs=(VMEM, VMEM),
        scratch_shapes=[
            pltpu.VMEM((3 * leaves, 2 * nv, 2 * rank), bf16),
            pltpu.VMEM((leaves, nv, rank), f32),
            pltpu.SemaphoreType.DMA,
        ],
        compiler_params=PARAMS,
        name="coupling",
    )(
        coupling_index.T, coeffs, coeff_across, coeff_beside, basis_in, own, coupling_blocks,
        *in_hbm(near_blocks),
    )

    return pl.pallas_call(
        last_kernel,
        out_shape=product,
        in_specs=[SMEM] * 2 + [VMEM] * 11,
        out_specs=VMEM,
        scratch_shapes=[pltpu.VMEM((3 * leaves, 2 * nv, 2 * points), bf16)],
        compiler_params=PARAMS,
        name="last",
    )(
        near_index.T, branch_index, vectors_in, vec_across, vec_beside, nodes, far_nodes, branch_blocks,
        cluster_transfer, folded, partial, first_blocks, other_blocks,
    )


def solution(mesh):
    lead = P(AXES)
    in_specs = (lead,) * 8 + (P("branch"),) * 2
    return jax.shard_map(per_device, mesh=mesh, in_specs=in_specs, out_specs=lead, check_vma=False)
```

```python
import jax
import jax.numpy as jnp
from jax import lax
from jax.experimental import pallas as pl
from jax.experimental.pallas import tpu as pltpu
from jax.sharding import PartitionSpec as P

AXES = ("branch", "sub")
f32, bf16 = jnp.float32, jnp.bfloat16
VMEM = pl.BlockSpec(memory_space=pltpu.VMEM)
SMEM = pl.BlockSpec(memory_space=pltpu.SMEM)
ANY = pl.BlockSpec(memory_space=pl.ANY)
PARAMS = pltpu.CompilerParams(vmem_limit_bytes=16 * 1024 * 1024)
CHUNKS = 2


def halves(x):
    high = x.astype(bf16)
    return high, (x - high.astype(f32)).astype(bf16)


def rows_of(x):
    high, low = halves(x)
    return jnp.concatenate(
        [jnp.concatenate([high, high], axis=1), jnp.concatenate([low, jnp.zeros_like(low)], axis=1)], axis=0
    )


def weights_of(w, axis):
    return jnp.concatenate(halves(w), axis=axis)


def both(x):
    n = x.shape[0] // 2
    return x[:n] + x[n:]


def dot_nt(a, b):
    return lax.dot_general(a, b, (((1,), (1,)), ((), ())), preferred_element_type=f32)


def dot_nn(a, b):
    return lax.dot_general(a, b, (((1,), (0,)), ((), ())), preferred_element_type=f32)


def pack(x):
    n = x.shape[0] // 2
    return jnp.concatenate([x[:n], x[n:]], axis=1)


def unpack(x):
    w = x.shape[1] // 2
    return jnp.concatenate([x[:, :w], x[:, w:]], axis=0)


def stream(sources, targets, sems):
    chunks = sems.shape[0]
    size = targets[0].shape[0] // chunks
    parts = []
    for c in range(chunks):
        part = pl.ds(c * size, size)
        copies = [
            pltpu.make_async_copy(src.at[part], dst.at[part], sems.at[c, i])
            for i, (src, dst) in enumerate(zip(sources, targets))
        ]
        for copy in copies:
            copy.start()
        parts.append((range(c * size, (c + 1) * size), copies))
    return parts


def then(body):
    pl.when(lax.axis_index("sub") >= 0)(body)


def wait_all(copies):
    for copy in copies:
        copy.wait()


def three(dot, a, weight):
    n = a.shape[0]
    rows = jnp.concatenate(halves(a), axis=0)
    high, low = halves(weight)
    wide = dot(rows, high)
    return wide[:n] + wide[n:] + dot(rows[:n], low)


def up_kernel(
    vectors_hbm, basis_hbm, transfer_hbm, top_hbm, blocks_hbm,
    share, folded, vectors, basis, blocks, transfer, top, sems, top_sem, block_sem,
):
    leaves, rank, points = basis.shape
    parts = stream((basis_hbm, transfer_hbm, vectors_hbm), (basis, transfer, vectors), sems)
    top_copy = pltpu.make_async_copy(top_hbm, top, top_sem)
    top_copy.start()
    block_copy = pltpu.make_async_copy(blocks_hbm.at[:, 0], blocks, block_sem)
    block_copy.start()

    @then
    def _():
        cluster = None
        for part, copies in parts:
            wait_all(copies)
            for l in part:
                high, low = halves(three(dot_nn, transfer[l], basis[l]))
                folded[l // 2, :, (l % 2) * points : (l % 2 + 1) * points] = jnp.concatenate([high, low, high], axis=0)
            for first in part[::2]:
                rows, weights = [], []
                for l in (first, first + 1):
                    lane = pl.ds((l % 2) * points, points)
                    weights += [folded[l // 2, :rank, lane], folded[l // 2, rank : 2 * rank, lane]]
                    rows.append(rows_of(vectors[l]))
                term = dot_nt(jnp.concatenate(rows, axis=1), jnp.concatenate(weights, axis=1))
                cluster = term if cluster is None else cluster + term
        top_copy.wait()
        share[...] = pack(three(dot_nt, both(cluster), top[0]))

    block_copy.wait()


def coeffs_kernel(vectors, basis, coeffs):
    half = coeffs.shape[0]
    for j in range(half):
        pair = [both(dot_nt(rows_of(vectors[l]), weights_of(basis[l], 1))) for l in (j, j + half)]
        coeffs[j] = jnp.concatenate(pair, axis=1)


def sides(own, across, beside):
    n = own[1]
    odd = lax.rem(lax.axis_index("sub"), 2)
    return (own[0], n), (beside, 2 * n * (1 - odd)), (across, 2 * n * odd)


def first_leaf(leaves):
    return (lax.axis_index("branch") * lax.axis_size("sub") + lax.axis_index("sub")) * leaves - leaves


def turned_sum(rows, blocks):
    weights = jnp.concatenate([weights_of(block, 1) for block in blocks], axis=1)
    return both(dot_nt(weights, jnp.concatenate(rows, axis=1)).T)


def dot_tn(a, b):
    return lax.dot_general(a, b, (((0,), (0,)), ((), ())), preferred_element_type=f32)


def own_kernel(vectors, blocks, branch_blocks, top, out, down):
    high, low = halves(top[0])
    for k in range(branch_blocks.shape[1]):
        first, second = halves(branch_blocks[0, k])
        down[k] = dot_tn(first, high) + dot_tn(second, high) + dot_tn(first, low)
    for l in range(blocks.shape[0]):
        out[l] = turned_sum([rows_of(vectors[l])], [blocks[l]])


def weights_kernel(blocks, out):
    for l in range(blocks.shape[0]):
        out[l] = jnp.concatenate([weights_of(blocks[l, k], 1) for k in range(blocks.shape[1])], axis=1)


def coupling_kernel(
    index, coeffs, across, beside, basis, near, blocks, out, split, far
):
    leaves, (coup, rank) = basis.shape[0], (index.shape[0], basis.shape[1])
    @then
    def _():
        half = leaves // 2
        left = lax.broadcasted_iota(jnp.int32, coeffs.shape[1:], 1) < rank
        for ref, base in sides((coeffs, leaves), across, beside):
            for j in range(half):
                two = ref[j]
                turned = pltpu.roll(two, rank, 1)
                for l, twice in ((j, jnp.where(left, two, turned)), (j + half, jnp.where(left, turned, two))):
                    high = twice.astype(bf16)
                    low = jnp.where(left, twice - high.astype(f32), 0.0).astype(bf16)
                    split[base + l] = jnp.concatenate([high, low], axis=0)
        anchor = first_leaf(leaves)
        for l in range(leaves):
            rows = jnp.concatenate([split[index[k, l] - anchor] for k in range(coup)], axis=1)
            weights = blocks[l]
            far[l] = both(dot_nt(rows, weights))
        for l in range(leaves):
            out[l] = near[l] + three(dot_nn, far[l], basis[l])

def last_kernel(
    near_index, branch_index, vectors, across, beside, nodes, far_nodes, steps, folded, partial, blocks,
    out_hbm, split, out, sems,
):
    leaves, near, points = blocks.shape[:3]
    branch = lax.axis_index("branch")
    known = nodes.shape[0]
    far = None
    for k in range(steps.shape[0]):
        slot = jnp.bitwise_xor(branch_index[0, k], branch)
        place = lax.rem(slot, known)
        node = unpack(jnp.where(slot < known, nodes[place], far_nodes[place]))
        term = three(dot_nn, node, steps[k])
        far = term if far is None else far + term
    high, low = halves(far)
    down = jnp.concatenate([high, high, low], axis=1)
    for ref, base in sides((vectors, leaves), across, beside):
        for l in range(leaves):
            split[base + l] = rows_of(ref[l])
    anchor = first_leaf(leaves)
    size, copies = leaves // sems.shape[0], []
    for l in range(leaves):
        if l % 2 == 0:
            two = dot_nn(down, folded[l // 2])
        rows = [split[near_index[k, l] - anchor] for k in range(1, near)]
        others = turned_sum(rows, [blocks[l, k] for k in range(1, near)])
        out[l] = partial[l] + others + two[:, (l % 2) * points : (l % 2 + 1) * points]
        if (l + 1) % size == 0:
            part = pl.ds(l + 1 - size, size)
            copies.append(pltpu.make_async_copy(out.at[part], out_hbm.at[part], sems.at[l // size]))
            copies[-1].start()
    wait_all(copies)


def in_hbm(*arrays):
    return [pltpu.with_memory_space_constraint(x, pltpu.HBM) for x in arrays]


def flip(x, mask, count):
    return lax.ppermute(x, AXES, [(i, i ^ mask) for i in range(count)])


def across_chips(beside, count):
    pairs = [(i, i + 2) for i in range(0, count - 2, 2)] + [(i + 3, i + 1) for i in range(0, count - 2, 2)]
    return lax.ppermute(beside, AXES, pairs + [(count - 2, count - 1), (1, 0)])


def per_device(
    vectors,
    leaf_basis,
    near_index,
    near_blocks,
    coupling_index,
    coupling_blocks,
    leaf_transfer,
    cluster_transfer,
    branch_index,
    branch_blocks,
):
    leaves, nv, points = vectors.shape
    rank = leaf_basis.shape[1]
    near = near_blocks.shape[1]
    half = leaves // 2
    members, branches = lax.axis_size("sub"), lax.axis_size("branch")
    count = members * branches
    sds = jax.ShapeDtypeStruct
    product = sds((leaves, nv, points), f32)

    vec_beside = flip(vectors, 1, count)

    share, folded, vectors_in, basis_in, own_blocks = pl.pallas_call(
        up_kernel,
        out_shape=(
            sds((nv // 2, 2 * rank), f32),
            sds((half, 3 * rank, 2 * points), bf16),
            product,
            sds(leaf_basis.shape, f32),
            sds((leaves, points, points), f32),
        ),
        in_specs=[ANY] * 5,
        out_specs=(VMEM,) * 5,
        scratch_shapes=[
            pltpu.VMEM(leaf_transfer.shape, f32),
            pltpu.VMEM(cluster_transfer.shape, f32),
            pltpu.SemaphoreType.DMA((CHUNKS, 3)),
            pltpu.SemaphoreType.DMA,
            pltpu.SemaphoreType.DMA,
        ],
        compiler_params=PARAMS,
        name="up",
    )(*in_hbm(vectors, leaf_basis, leaf_transfer, cluster_transfer, near_blocks))

    first = flip(share, 1, count)
    coeffs = pl.pallas_call(
        coeffs_kernel,
        out_shape=sds((half, nv, 2 * rank), f32),
        in_specs=[VMEM] * 2,
        out_specs=VMEM,
        compiler_params=PARAMS,
        name="coeffs",
    )(vectors_in, basis_in)
    coeff_beside = flip(coeffs, 1, count)
    node = share + first
    node, coeffs = lax.optimization_barrier((node, coeffs))
    own, down = pl.pallas_call(
        own_kernel,
        out_shape=(product, sds(branch_blocks.shape[1:], f32)),
        in_specs=[VMEM] * 4,
        out_specs=(VMEM, VMEM),
        compiler_params=PARAMS,
        name="near_own",
    )(vectors_in, own_blocks, branch_blocks, cluster_transfer)

    bit = 2
    while bit < members:
        node = node + flip(node, bit + 1, count)
        bit *= 2
    coeff_across = across_chips(coeff_beside, count)
    nodes = node[None]
    vec_across = across_chips(vec_beside, count)
    while 2 * bit < count:
        if 4 * bit == count:
            nodes, own = lax.optimization_barrier((nodes, own))
        nodes = jnp.concatenate([nodes, flip(nodes, bit + 1, count)], axis=0)
        bit *= 2
    weights = pl.pallas_call(
        weights_kernel,
        out_shape=sds((leaves, rank, 2 * coupling_blocks.shape[1] * rank), bf16),
        in_specs=[VMEM],
        out_specs=VMEM,
        compiler_params=PARAMS,
        name="coupling_weights",
    )(coupling_blocks)
    nodes, weights = lax.optimization_barrier((nodes, weights))
    far_nodes = flip(nodes, bit + 1, count)

    partial = pl.pallas_call(
        coupling_kernel,
        out_shape=product,
        in_specs=[SMEM] + [VMEM] * 6,
        out_specs=VMEM,
        scratch_shapes=[
            pltpu.VMEM((3 * leaves, 2 * nv, 2 * rank), bf16),
            pltpu.VMEM((leaves, nv, rank), f32),
        ],
        compiler_params=PARAMS,
        name="coupling",
    )(
        coupling_index.T, coeffs, coeff_across, coeff_beside, basis_in, own, weights,
    )

    return pl.pallas_call(
        last_kernel,
        out_shape=product,
        in_specs=[SMEM] * 2 + [VMEM] * 9,
        out_specs=ANY,
        scratch_shapes=[
            pltpu.VMEM((3 * leaves, 2 * nv, 2 * points), bf16),
            pltpu.VMEM((leaves, nv, points), f32),
            pltpu.SemaphoreType.DMA((3,)),
        ],
        compiler_params=PARAMS,
        name="last",
    )(
        near_index.T, branch_index, vectors_in, vec_across, vec_beside, nodes, far_nodes, down,
        folded, partial, near_blocks,
    )


def solution(mesh):
    lead = P(AXES)
    in_specs = (lead,) * 8 + (P("branch"),) * 2
    return jax.shard_map(per_device, mesh=mesh, in_specs=in_specs, out_specs=lead, check_vma=False)
```

```python
import jax
import jax.numpy as jnp
from jax import lax
from jax.experimental import pallas as pl
from jax.experimental.pallas import tpu as pltpu
from jax.sharding import PartitionSpec as P

AXES = ("branch", "sub")
f32, bf16 = jnp.float32, jnp.bfloat16
VMEM = pl.BlockSpec(memory_space=pltpu.VMEM)
SMEM = pl.BlockSpec(memory_space=pltpu.SMEM)
ANY = pl.BlockSpec(memory_space=pl.ANY)
PARAMS = pltpu.CompilerParams(vmem_limit_bytes=16 * 1024 * 1024)
CHUNKS = 2


def halves(x):
    high = x.astype(bf16)
    return high, (x - high.astype(f32)).astype(bf16)


def rows_of(x):
    high, low = halves(x)
    return jnp.concatenate(
        [jnp.concatenate([high, high], axis=1), jnp.concatenate([low, jnp.zeros_like(low)], axis=1)], axis=0
    )


def weights_of(w, axis):
    return jnp.concatenate(halves(w), axis=axis)


def both(x):
    n = x.shape[0] // 2
    return x[:n] + x[n:]


def dot_nt(a, b):
    return lax.dot_general(a, b, (((1,), (1,)), ((), ())), preferred_element_type=f32)


def dot_nn(a, b):
    return lax.dot_general(a, b, (((1,), (0,)), ((), ())), preferred_element_type=f32)


def pack(x):
    n = x.shape[0] // 2
    return jnp.concatenate([x[:n], x[n:]], axis=1)


def unpack(x):
    w = x.shape[1] // 2
    return jnp.concatenate([x[:, :w], x[:, w:]], axis=0)


def stream(sources, targets, sems):
    chunks = sems.shape[0]
    size = targets[0].shape[0] // chunks
    parts = []
    for c in range(chunks):
        part = pl.ds(c * size, size)
        copies = [
            pltpu.make_async_copy(src.at[part], dst.at[part], sems.at[c, i])
            for i, (src, dst) in enumerate(zip(sources, targets))
        ]
        for copy in copies:
            copy.start()
        parts.append((range(c * size, (c + 1) * size), copies))
    return parts


def then(body):
    pl.when(lax.axis_index("sub") >= 0)(body)


def wait_all(copies):
    for copy in copies:
        copy.wait()


def three(dot, a, weight):
    n = a.shape[0]
    rows = jnp.concatenate(halves(a), axis=0)
    high, low = halves(weight)
    wide = dot(rows, high)
    return wide[:n] + wide[n:] + dot(rows[:n], low)


def up_kernel(
    vectors_hbm, basis_hbm, transfer_hbm, top_hbm, blocks_hbm,
    share, folded, vectors, basis, blocks, transfer, top, sems, top_sem, block_sem,
):
    leaves, rank, points = basis.shape
    parts = stream((basis_hbm, transfer_hbm, vectors_hbm), (basis, transfer, vectors), sems)
    top_copy = pltpu.make_async_copy(top_hbm, top, top_sem)
    top_copy.start()
    block_copy = pltpu.make_async_copy(blocks_hbm.at[:, 0], blocks, block_sem)
    block_copy.start()

    @then
    def _():
        cluster = None
        for part, copies in parts:
            wait_all(copies)
            for l in part:
                high, low = halves(three(dot_nn, transfer[l], basis[l]))
                folded[l // 2, :, (l % 2) * points : (l % 2 + 1) * points] = jnp.concatenate([high, low, high], axis=0)
            for first in part[::2]:
                rows, weights = [], []
                for l in (first, first + 1):
                    lane = pl.ds((l % 2) * points, points)
                    weights += [folded[l // 2, :rank, lane], folded[l // 2, rank : 2 * rank, lane]]
                    rows.append(rows_of(vectors[l]))
                term = dot_nt(jnp.concatenate(rows, axis=1), jnp.concatenate(weights, axis=1))
                cluster = term if cluster is None else cluster + term
        top_copy.wait()
        share[...] = pack(three(dot_nt, both(cluster), top[0]))

    block_copy.wait()


def coeffs_kernel(vectors, basis, coeffs):
    half = coeffs.shape[0]
    for j in range(half):
        pair = [both(dot_nt(rows_of(vectors[l]), weights_of(basis[l], 1))) for l in (j, j + half)]
        coeffs[j] = jnp.concatenate(pair, axis=1)


def sides(own, across, beside):
    n = own[1]
    odd = lax.rem(lax.axis_index("sub"), 2)
    return (own[0], n), (beside, 2 * n * (1 - odd)), (across, 2 * n * odd)


def first_leaf(leaves):
    return (lax.axis_index("branch") * lax.axis_size("sub") + lax.axis_index("sub")) * leaves - leaves


def turned_sum(rows, blocks):
    weights = jnp.concatenate([weights_of(block, 1) for block in blocks], axis=1)
    return both(dot_nt(weights, jnp.concatenate(rows, axis=1)).T)


def dot_tn(a, b):
    return lax.dot_general(a, b, (((0,), (0,)), ((), ())), preferred_element_type=f32)


def own_kernel(vectors, blocks, branch_blocks, top, out, down):
    high, low = halves(top[0])
    for k in range(branch_blocks.shape[1]):
        first, second = halves(branch_blocks[0, k])
        down[k] = dot_tn(first, high) + dot_tn(second, high) + dot_tn(first, low)
    for l in range(blocks.shape[0]):
        out[l] = turned_sum([rows_of(vectors[l])], [blocks[l]])


def weights_kernel(blocks, out):
    for l in range(blocks.shape[0]):
        out[l] = jnp.concatenate([weights_of(blocks[l, k], 1) for k in range(blocks.shape[1])], axis=1)


def coupling_kernel(
    index, coeffs, across, beside, basis, near, blocks, out, split, far
):
    leaves, (coup, rank) = basis.shape[0], (index.shape[0], basis.shape[1])
    @then
    def _():
        half = leaves // 2
        left = lax.broadcasted_iota(jnp.int32, coeffs.shape[1:], 1) < rank
        for ref, base in sides((coeffs, leaves), across, beside):
            for j in range(half):
                two = ref[j]
                turned = pltpu.roll(two, rank, 1)
                for l, twice in ((j, jnp.where(left, two, turned)), (j + half, jnp.where(left, turned, two))):
                    high = twice.astype(bf16)
                    low = jnp.where(left, twice - high.astype(f32), 0.0).astype(bf16)
                    split[base + l] = jnp.concatenate([high, low], axis=0)
        anchor = first_leaf(leaves)
        for l in range(leaves):
            rows = jnp.concatenate([split[index[k, l] - anchor] for k in range(coup)], axis=1)
            weights = blocks[l]
            far[l] = both(dot_nt(rows, weights))
        for l in range(leaves):
            out[l] = near[l] + three(dot_nn, far[l], basis[l])

def last_kernel(
    near_index, branch_index, vectors, across, beside, nodes, far_nodes, steps, folded, partial, blocks,
    out_hbm, split, out, sems,
):
    leaves, near, points = blocks.shape[:3]
    branch = lax.axis_index("branch")
    known = nodes.shape[0]
    far = None
    for k in range(steps.shape[0]):
        slot = jnp.bitwise_xor(branch_index[0, k], branch)
        place = lax.rem(slot, known)
        node = unpack(jnp.where(slot < known, nodes[place], far_nodes[place]))
        term = three(dot_nn, node, steps[k])
        far = term if far is None else far + term
    high, low = halves(far)
    down = jnp.concatenate([high, high, low], axis=1)
    for ref, base in sides((vectors, leaves), across, beside):
        for l in range(leaves):
            split[base + l] = rows_of(ref[l])
    anchor = first_leaf(leaves)
    size, copies, lag = leaves // sems.shape[0], [], leaves // 3
    for step in range(leaves + lag):
        if step < leaves:
            rows = [split[near_index[k, step] - anchor] for k in range(1, near)]
            out[step] = partial[step] + turned_sum(rows, [blocks[step, k] for k in range(1, near)])
        l = step - lag
        if l >= 0:
            if l % 2 == 0:
                two = dot_nn(down, folded[l // 2])
            out[l] = out[l] + two[:, (l % 2) * points : (l % 2 + 1) * points]
            if (l + 1) % size == 0:
                part = pl.ds(l + 1 - size, size)
                copies.append(pltpu.make_async_copy(out.at[part], out_hbm.at[part], sems.at[l // size]))
                copies[-1].start()
    wait_all(copies)


def in_hbm(*arrays):
    return [pltpu.with_memory_space_constraint(x, pltpu.HBM) for x in arrays]


def flip(x, mask, count):
    return lax.ppermute(x, AXES, [(i, i ^ mask) for i in range(count)])


def across_chips(beside, count):
    pairs = [(i, i + 2) for i in range(0, count - 2, 2)] + [(i + 3, i + 1) for i in range(0, count - 2, 2)]
    return lax.ppermute(beside, AXES, pairs + [(count - 2, count - 1), (1, 0)])


def per_device(
    vectors,
    leaf_basis,
    near_index,
    near_blocks,
    coupling_index,
    coupling_blocks,
    leaf_transfer,
    cluster_transfer,
    branch_index,
    branch_blocks,
):
    leaves, nv, points = vectors.shape
    rank = leaf_basis.shape[1]
    near = near_blocks.shape[1]
    half = leaves // 2
    members, branches = lax.axis_size("sub"), lax.axis_size("branch")
    count = members * branches
    sds = jax.ShapeDtypeStruct
    product = sds((leaves, nv, points), f32)

    vec_beside = flip(vectors, 1, count)

    share, folded, vectors_in, basis_in, own_blocks = pl.pallas_call(
        up_kernel,
        out_shape=(
            sds((nv // 2, 2 * rank), f32),
            sds((half, 3 * rank, 2 * points), bf16),
            product,
            sds(leaf_basis.shape, f32),
            sds((leaves, points, points), f32),
        ),
        in_specs=[ANY] * 5,
        out_specs=(VMEM,) * 5,
        scratch_shapes=[
            pltpu.VMEM(leaf_transfer.shape, f32),
            pltpu.VMEM(cluster_transfer.shape, f32),
            pltpu.SemaphoreType.DMA((CHUNKS, 3)),
            pltpu.SemaphoreType.DMA,
            pltpu.SemaphoreType.DMA,
        ],
        compiler_params=PARAMS,
        name="up",
    )(*in_hbm(vectors, leaf_basis, leaf_transfer, cluster_transfer, near_blocks))

    first = flip(share, 1, count)
    coeffs = pl.pallas_call(
        coeffs_kernel,
        out_shape=sds((half, nv, 2 * rank), f32),
        in_specs=[VMEM] * 2,
        out_specs=VMEM,
        compiler_params=PARAMS,
        name="coeffs",
    )(vectors_in, basis_in)
    coeff_beside = flip(coeffs, 1, count)
    node = share + first
    node, coeffs = lax.optimization_barrier((node, coeffs))
    own, down = pl.pallas_call(
        own_kernel,
        out_shape=(product, sds(branch_blocks.shape[1:], f32)),
        in_specs=[VMEM] * 4,
        out_specs=(VMEM, VMEM),
        compiler_params=PARAMS,
        name="near_own",
    )(vectors_in, own_blocks, branch_blocks, cluster_transfer)

    bit = 2
    while bit < members:
        node = node + flip(node, bit + 1, count)
        bit *= 2
    coeff_across = across_chips(coeff_beside, count)
    nodes = node[None]
    vec_across = across_chips(vec_beside, count)
    while 2 * bit < count:
        if 4 * bit == count:
            nodes, own = lax.optimization_barrier((nodes, own))
        nodes = jnp.concatenate([nodes, flip(nodes, bit + 1, count)], axis=0)
        bit *= 2
    weights = pl.pallas_call(
        weights_kernel,
        out_shape=sds((leaves, rank, 2 * coupling_blocks.shape[1] * rank), bf16),
        in_specs=[VMEM],
        out_specs=VMEM,
        compiler_params=PARAMS,
        name="coupling_weights",
    )(coupling_blocks)
    nodes, weights = lax.optimization_barrier((nodes, weights))
    far_nodes = flip(nodes, bit + 1, count)

    partial = pl.pallas_call(
        coupling_kernel,
        out_shape=product,
        in_specs=[SMEM] + [VMEM] * 6,
        out_specs=VMEM,
        scratch_shapes=[
            pltpu.VMEM((3 * leaves, 2 * nv, 2 * rank), bf16),
            pltpu.VMEM((leaves, nv, rank), f32),
        ],
        compiler_params=PARAMS,
        name="coupling",
    )(
        coupling_index.T, coeffs, coeff_across, coeff_beside, basis_in, own, weights,
    )

    return pl.pallas_call(
        last_kernel,
        out_shape=product,
        in_specs=[SMEM] * 2 + [VMEM] * 9,
        out_specs=ANY,
        scratch_shapes=[
            pltpu.VMEM((3 * leaves, 2 * nv, 2 * points), bf16),
            pltpu.VMEM((leaves, nv, points), f32),
            pltpu.SemaphoreType.DMA((3,)),
        ],
        compiler_params=PARAMS,
        name="last",
    )(
        near_index.T, branch_index, vectors_in, vec_across, vec_beside, nodes, far_nodes, down,
        folded, partial, near_blocks,
    )


def solution(mesh):
    lead = P(AXES)
    in_specs = (lead,) * 8 + (P("branch"),) * 2
    return jax.shard_map(per_device, mesh=mesh, in_specs=in_specs, out_specs=lead, check_vma=False)
```

```python
import jax
import jax.numpy as jnp
from jax import lax
from jax.experimental import pallas as pl
from jax.experimental.pallas import tpu as pltpu
from jax.sharding import PartitionSpec as P

AXES = ("branch", "sub")
f32, bf16 = jnp.float32, jnp.bfloat16
VMEM = pl.BlockSpec(memory_space=pltpu.VMEM)
SMEM = pl.BlockSpec(memory_space=pltpu.SMEM)
ANY = pl.BlockSpec(memory_space=pl.ANY)
PARAMS = pltpu.CompilerParams(vmem_limit_bytes=16 * 1024 * 1024)
CHUNKS = 2


def halves(x):
    high = x.astype(bf16)
    return high, (x - high.astype(f32)).astype(bf16)


def rows_of(x):
    high, low = halves(x)
    return jnp.concatenate(
        [jnp.concatenate([high, high], axis=1), jnp.concatenate([low, jnp.zeros_like(low)], axis=1)], axis=0
    )


def weights_of(w, axis):
    return jnp.concatenate(halves(w), axis=axis)


def both(x):
    n = x.shape[0] // 2
    return x[:n] + x[n:]


def dot_nt(a, b):
    return lax.dot_general(a, b, (((1,), (1,)), ((), ())), preferred_element_type=f32)


def dot_nn(a, b):
    return lax.dot_general(a, b, (((1,), (0,)), ((), ())), preferred_element_type=f32)


def pack(x):
    n = x.shape[0] // 2
    return jnp.concatenate([x[:n], x[n:]], axis=1)


def unpack(x):
    w = x.shape[1] // 2
    return jnp.concatenate([x[:, :w], x[:, w:]], axis=0)


def stream(sources, targets, sems):
    chunks = sems.shape[0]
    size = targets[0].shape[0] // chunks
    parts = []
    for c in range(chunks):
        part = pl.ds(c * size, size)
        copies = [
            pltpu.make_async_copy(src.at[part], dst.at[part], sems.at[c, i])
            for i, (src, dst) in enumerate(zip(sources, targets))
        ]
        for copy in copies:
            copy.start()
        parts.append((range(c * size, (c + 1) * size), copies))
    return parts


def then(body):
    pl.when(lax.axis_index("sub") >= 0)(body)


def wait_all(copies):
    for copy in copies:
        copy.wait()


def three(dot, a, weight):
    n = a.shape[0]
    rows = jnp.concatenate(halves(a), axis=0)
    high, low = halves(weight)
    wide = dot(rows, high)
    return wide[:n] + wide[n:] + dot(rows[:n], low)


def up_kernel(
    vectors_hbm, basis_hbm, transfer_hbm, top_hbm, blocks_hbm,
    share, folded, vectors, basis, blocks, transfer, top, sems, top_sem, block_sem,
):
    leaves, rank, points = basis.shape
    parts = stream((basis_hbm, transfer_hbm, vectors_hbm), (basis, transfer, vectors), sems)
    top_copy = pltpu.make_async_copy(top_hbm, top, top_sem)
    top_copy.start()
    block_copy = pltpu.make_async_copy(blocks_hbm.at[:, 0], blocks, block_sem)
    block_copy.start()

    @then
    def _():
        cluster = None
        for part, copies in parts:
            wait_all(copies)
            for l in part:
                high, low = halves(three(dot_nn, transfer[l], basis[l]))
                folded[l // 2, :, (l % 2) * points : (l % 2 + 1) * points] = jnp.concatenate([high, low, high], axis=0)
            for first in part[::2]:
                rows, weights = [], []
                for l in (first, first + 1):
                    lane = pl.ds((l % 2) * points, points)
                    weights += [folded[l // 2, :rank, lane], folded[l // 2, rank : 2 * rank, lane]]
                    rows.append(rows_of(vectors[l]))
                term = dot_nt(jnp.concatenate(rows, axis=1), jnp.concatenate(weights, axis=1))
                cluster = term if cluster is None else cluster + term
        top_copy.wait()
        share[...] = pack(three(dot_nt, both(cluster), top[0]))

    block_copy.wait()


def coeffs_kernel(vectors, basis, coeffs):
    half = coeffs.shape[0]
    for j in range(half):
        pair = [both(dot_nt(rows_of(vectors[l]), weights_of(basis[l], 1))) for l in (j, j + half)]
        coeffs[j] = jnp.concatenate(pair, axis=1)


def sides(own, across, beside):
    n = own[1]
    odd = lax.rem(lax.axis_index("sub"), 2)
    return (own[0], n), (beside, 2 * n * (1 - odd)), (across, 2 * n * odd)


def first_leaf(leaves):
    return (lax.axis_index("branch") * lax.axis_size("sub") + lax.axis_index("sub")) * leaves - leaves


def turned_sum(rows, blocks):
    weights = jnp.concatenate([weights_of(block, 1) for block in blocks], axis=1)
    return both(dot_nt(weights, jnp.concatenate(rows, axis=1)).T)


def dot_tn(a, b):
    return lax.dot_general(a, b, (((0,), (0,)), ((), ())), preferred_element_type=f32)


def own_kernel(vectors, blocks, branch_blocks, top, out, down):
    high, low = halves(top[0])
    for k in range(branch_blocks.shape[1]):
        first, second = halves(branch_blocks[0, k])
        down[k] = dot_tn(first, high) + dot_tn(second, high) + dot_tn(first, low)
    for l in range(blocks.shape[0]):
        out[l] = turned_sum([rows_of(vectors[l])], [blocks[l]])


def weights_kernel(blocks, basis, out, basis_out):
    for l in range(blocks.shape[0]):
        basis_out[l] = weights_of(basis[l], 0)
        out[l] = jnp.concatenate([weights_of(blocks[l, k], 1) for k in range(blocks.shape[1])], axis=1)


def coupling_kernel(
    index, coeffs, across, beside, basis, near, blocks, out, split, far
):
    leaves, coup, rank, nv = basis.shape[0], index.shape[0], basis.shape[1] // 2, out.shape[1]
    @then
    def _():
        half = leaves // 2
        left = lax.broadcasted_iota(jnp.int32, coeffs.shape[1:], 1) < rank
        for ref, base in sides((coeffs, leaves), across, beside):
            for j in range(half):
                two = ref[j]
                turned = pltpu.roll(two, rank, 1)
                for l, twice in ((j, jnp.where(left, two, turned)), (j + half, jnp.where(left, turned, two))):
                    high = twice.astype(bf16)
                    low = jnp.where(left, twice - high.astype(f32), 0.0).astype(bf16)
                    split[base + l] = jnp.concatenate([high, low], axis=0)
        anchor = first_leaf(leaves)
        for l in range(leaves):
            rows = jnp.concatenate([split[index[k, l] - anchor] for k in range(coup)], axis=1)
            weights = blocks[l]
            far[l] = both(dot_nt(rows, weights))
        for l in range(leaves):
            rows = jnp.concatenate(halves(far[l]), axis=0)
            wide = dot_nn(rows, basis[l, :rank])
            out[l] = near[l] + wide[:nv] + wide[nv:] + dot_nn(rows[:nv], basis[l, rank:])

def last_kernel(
    near_index, branch_index, vectors, across, beside, nodes, far_nodes, steps, folded, partial, blocks,
    out_hbm, split, out, sems,
):
    leaves, near, points = blocks.shape[:3]
    branch = lax.axis_index("branch")
    known = nodes.shape[0]
    far = None
    for k in range(steps.shape[0]):
        slot = jnp.bitwise_xor(branch_index[0, k], branch)
        place = lax.rem(slot, known)
        node = unpack(jnp.where(slot < known, nodes[place], far_nodes[place]))
        term = three(dot_nn, node, steps[k])
        far = term if far is None else far + term
    high, low = halves(far)
    down = jnp.concatenate([high, high, low], axis=1)
    for ref, base in sides((vectors, leaves), across, beside):
        for l in range(leaves):
            split[base + l] = rows_of(ref[l])
    anchor = first_leaf(leaves)
    size, copies, lag = leaves // sems.shape[0], [], leaves // 3
    for step in range(leaves + lag):
        if step < leaves:
            rows = [split[near_index[k, step] - anchor] for k in range(1, near)]
            out[step] = partial[step] + turned_sum(rows, [blocks[step, k] for k in range(1, near)])
        l = step - lag
        if l >= 0:
            if l % 2 == 0:
                two = dot_nn(down, folded[l // 2])
            out[l] = out[l] + two[:, (l % 2) * points : (l % 2 + 1) * points]
            if (l + 1) % size == 0:
                part = pl.ds(l + 1 - size, size)
                copies.append(pltpu.make_async_copy(out.at[part], out_hbm.at[part], sems.at[l // size]))
                copies[-1].start()
    wait_all(copies)


def in_hbm(*arrays):
    return [pltpu.with_memory_space_constraint(x, pltpu.HBM) for x in arrays]


def flip(x, mask, count):
    return lax.ppermute(x, AXES, [(i, i ^ mask) for i in range(count)])


def across_chips(beside, count):
    pairs = [(i, i + 2) for i in range(0, count - 2, 2)] + [(i + 3, i + 1) for i in range(0, count - 2, 2)]
    return lax.ppermute(beside, AXES, pairs + [(count - 2, count - 1), (1, 0)])


def per_device(
    vectors,
    leaf_basis,
    near_index,
    near_blocks,
    coupling_index,
    coupling_blocks,
    leaf_transfer,
    cluster_transfer,
    branch_index,
    branch_blocks,
):
    leaves, nv, points = vectors.shape
    rank = leaf_basis.shape[1]
    near = near_blocks.shape[1]
    half = leaves // 2
    members, branches = lax.axis_size("sub"), lax.axis_size("branch")
    count = members * branches
    sds = jax.ShapeDtypeStruct
    product = sds((leaves, nv, points), f32)

    vec_beside = flip(vectors, 1, count)

    share, folded, vectors_in, basis_in, own_blocks = pl.pallas_call(
        up_kernel,
        out_shape=(
            sds((nv // 2, 2 * rank), f32),
            sds((half, 3 * rank, 2 * points), bf16),
            product,
            sds(leaf_basis.shape, f32),
            sds((leaves, points, points), f32),
        ),
        in_specs=[ANY] * 5,
        out_specs=(VMEM,) * 5,
        scratch_shapes=[
            pltpu.VMEM(leaf_transfer.shape, f32),
            pltpu.VMEM(cluster_transfer.shape, f32),
            pltpu.SemaphoreType.DMA((CHUNKS, 3)),
            pltpu.SemaphoreType.DMA,
            pltpu.SemaphoreType.DMA,
        ],
        compiler_params=PARAMS,
        name="up",
    )(*in_hbm(vectors, leaf_basis, leaf_transfer, cluster_transfer, near_blocks))

    first = flip(share, 1, count)
    coeffs = pl.pallas_call(
        coeffs_kernel,
        out_shape=sds((half, nv, 2 * rank), f32),
        in_specs=[VMEM] * 2,
        out_specs=VMEM,
        compiler_params=PARAMS,
        name="coeffs",
    )(vectors_in, basis_in)
    coeff_beside = flip(coeffs, 1, count)
    node = share + first
    node, coeffs = lax.optimization_barrier((node, coeffs))
    own, down = pl.pallas_call(
        own_kernel,
        out_shape=(product, sds(branch_blocks.shape[1:], f32)),
        in_specs=[VMEM] * 4,
        out_specs=(VMEM, VMEM),
        compiler_params=PARAMS,
        name="near_own",
    )(vectors_in, own_blocks, branch_blocks, cluster_transfer)

    bit = 2
    while bit < members:
        node = node + flip(node, bit + 1, count)
        bit *= 2
    coeff_across = across_chips(coeff_beside, count)
    nodes = node[None]
    vec_across = across_chips(vec_beside, count)
    while 2 * bit < count:
        if 4 * bit == count:
            nodes, own = lax.optimization_barrier((nodes, own))
        nodes = jnp.concatenate([nodes, flip(nodes, bit + 1, count)], axis=0)
        bit *= 2
    weights, basis_parts = pl.pallas_call(
        weights_kernel,
        out_shape=(
            sds((leaves, rank, 2 * coupling_blocks.shape[1] * rank), bf16),
            sds((leaves, 2 * rank, points), bf16),
        ),
        in_specs=[VMEM] * 2,
        out_specs=(VMEM, VMEM),
        compiler_params=PARAMS,
        name="coupling_weights",
    )(coupling_blocks, basis_in)
    nodes, weights = lax.optimization_barrier((nodes, weights))
    far_nodes = flip(nodes, bit + 1, count)

    partial = pl.pallas_call(
        coupling_kernel,
        out_shape=product,
        in_specs=[SMEM] + [VMEM] * 6,
        out_specs=VMEM,
        scratch_shapes=[
            pltpu.VMEM((3 * leaves, 2 * nv, 2 * rank), bf16),
            pltpu.VMEM((leaves, nv, rank), f32),
        ],
        compiler_params=PARAMS,
        name="coupling",
    )(
        coupling_index.T, coeffs, coeff_across, coeff_beside, basis_parts, own, weights,
    )

    return pl.pallas_call(
        last_kernel,
        out_shape=product,
        in_specs=[SMEM] * 2 + [VMEM] * 9,
        out_specs=ANY,
        scratch_shapes=[
            pltpu.VMEM((3 * leaves, 2 * nv, 2 * points), bf16),
            pltpu.VMEM((leaves, nv, points), f32),
            pltpu.SemaphoreType.DMA((3,)),
        ],
        compiler_params=PARAMS,
        name="last",
    )(
        near_index.T, branch_index, vectors_in, vec_across, vec_beside, nodes, far_nodes, down,
        folded, partial, near_blocks,
    )


def solution(mesh):
    lead = P(AXES)
    in_specs = (lead,) * 8 + (P("branch"),) * 2
    return jax.shard_map(per_device, mesh=mesh, in_specs=in_specs, out_specs=lead, check_vma=False)
```
